512 devices in a mesh: lat: 32 (over x, z_lo, core), lon: 16 (over z_hi, y).
Axes of the slice: x: 4, y: 8, z: 8 (z_hi: 2, z_lo: 4; z = z_hi * 4 + z_lo), core: 2. Of those that a mesh axis runs over, the one named last changes fastest.
Arguments:
- fields: bfloat16 [256, 64, 1440], P(None, 'lat', 'lon'), may hold values from -6 to 6
- basis: bfloat16 [64, 3, 9, 128], replicated, may hold values from -0.3125 to 0.3125
- half_width: int32 [64], replicated, may hold values from 1 to 64, as said below
- weight: bfloat16 [256, 9, 256], replicated, may hold values from -0.125 to 0.125
- cotangent: bfloat16 [256, 64, 1440], P(None, 'lat', 'lon'), may hold values from -6 to 6
Outputs:
- output: bfloat16 [256, 64, 1440], P(None, 'lat', 'lon')
- input_grad: bfloat16 [256, 64, 1440], P(None, 'lat', 'lon')
- weight_grad: float32 [589824], P(('lat', 'lon'))
The draws below stay inside these ranges and needn't reach their ends.
Inputs may be any that keep to these rules, and one draw needn't show every extreme that they name: `half_width`: row i lies at colatitude i quarter degrees; row 0 is the pole and has half-width 64; away from the pole the half-width shrinks about as one over the sine of the colatitude, with small random increments.
All inputs are finite; a program needn't handle non-finite values.
Results may differ from the reference program's by a relative error of at most 0.007.
Values may be sent and summed in bfloat16 or wider, within the bound.
A program may use at most 64 MiB of HBM per device.

```python
import math
import jax
import jax.numpy as jnp
import numpy as np
from jax import lax

CHAN = 256
BASIS = 9
NLON = 1440
REACH = 64
TAPS = 128
NLAT = 64


def draw_half_width(key, part):
    key = jax.random.fold_in(key, 11)
    row_ids = np.arange(NLAT)
    sines = np.sin(row_ids * math.pi / 720.0)
    far_sine = math.sin((NLAT - 1) * math.pi / 720.0)
    spread = np.ceil(REACH * far_sine / (4.0 * np.maximum(sines, 1e-12)))
    table = np.where(sines > 0, np.minimum(spread, REACH), REACH).astype(np.int32)
    narrow = max(1, REACH // 8)
    jitter = jax.random.randint(key, (NLAT,), 0, narrow + 1, dtype=jnp.int32)
    return jnp.clip(jnp.asarray(table, dtype=jnp.int32) + jitter, 1, REACH).astype(jnp.int32)


def block_scale(key, extent, cuts, least, high):
    loudness = 1.0
    for position, parts in cuts:
        draws = jax.random.uniform(jax.random.fold_in(jax.random.fold_in(key, 6), position), (parts,), jnp.float32, least / len(cuts), high / len(cuts))
        loudness = loudness * jnp.repeat(jnp.exp(draws), extent[position] // parts).reshape((-1,) + (1,) * (len(extent) - 1 - position))
    return loudness


def scatter_about(key, extent, scale, limit, cuts=(), held_as=jnp.bfloat16):
    gain = block_scale(key, extent, cuts, -0.22, 0.18) if cuts else 1.0
    values = jax.random.normal(key, extent, jnp.float32) * scale * gain
    return jnp.minimum(jnp.maximum(values, -limit), limit).astype(held_as)


def setup_inputs(seed: int = 0) -> dict:
    key_of = jax.random.split(jax.random.key(seed), 6)
    return {
        "fields": scatter_about(key_of[0], (CHAN, NLAT, NLON), 1.0, 6.0, ((1, 32), (2, 16))),
        "basis": scatter_about(key_of[1], (NLAT, 3, BASIS, TAPS), (6 * REACH) ** -0.5, 0.3125),
        "half_width": draw_half_width(jax.random.fold_in(key_of[5], 71), 0),
        "weight": scatter_about(key_of[3], (CHAN, BASIS, CHAN), (CHAN * BASIS) ** -0.5, 0.125),
        "cotangent": scatter_about(key_of[4], (CHAN, NLAT, NLON), 1.0, 6.0, ((1, 32), (2, 16))),
    }


def correlate(stencil_rows, kernel):
    result = lax.conv_general_dilated(stencil_rows, jnp.transpose(kernel, (1, 0, 2)), (1,), 'VALID', dimension_numbers=('NCW', 'OIW', 'NCW'), precision=lax.Precision.HIGHEST)
    return result[:, :, :NLON]

def reference(fields, basis, half_width, weight, cotangent):
    tap_offset = jnp.arange(TAPS, dtype=jnp.int32) - REACH
    inside = jnp.abs(tap_offset)[None, :] <= half_width[:, None]
    masked = jnp.where(inside[:, None, None, :], basis, jnp.zeros_like(basis))
    masked_wide = masked.astype(jnp.float32)
    weight_wide = weight.astype(jnp.float32)
    wrapped = jnp.concatenate([fields[:, :, NLON - REACH:], fields, fields[:, :, :REACH]], axis=2).astype(jnp.float32)
    padded = jnp.pad(wrapped, ((0, 0), (1, 1), (0, 0)))

    def per_row(carried, row_index):
        grad_sum, back_sum = carried
        stencil_rows = lax.dynamic_slice_in_dim(padded, row_index, 3, 1)
        kernel = masked_wide[row_index]
        projected = correlate(stencil_rows, kernel).astype(jnp.bfloat16)
        projected_wide = projected.astype(jnp.float32)
        mixed_row = jnp.einsum('okc,ckj->oj', weight_wide, projected_wide, precision=lax.Precision.HIGHEST).astype(jnp.bfloat16)
        cot_row = lax.dynamic_index_in_dim(cotangent, row_index, 1, keepdims=False).astype(jnp.float32)
        grad_sum = grad_sum + jnp.einsum('oj,ckj->okc', cot_row, projected_wide, precision=lax.Precision.HIGHEST)
        grad_mix = jnp.einsum('okc,oj->ckj', weight_wide, cot_row, precision=lax.Precision.HIGHEST).astype(jnp.bfloat16)
        grad_mix = lax.optimization_barrier(grad_mix).astype(jnp.float32)
        _, pullback = jax.vjp(lambda rows_in: correlate(rows_in, kernel), stencil_rows)
        spread, = pullback(grad_mix)
        window = lax.dynamic_slice_in_dim(back_sum, row_index, 3, 1)
        back_sum = lax.dynamic_update_slice_in_dim(back_sum, window + spread, row_index, 1)
        return ((grad_sum, back_sum), mixed_row)
    start_grad = jnp.zeros((CHAN, BASIS, CHAN), jnp.float32)
    start_back = jnp.zeros((CHAN, NLAT + 2, NLON + 2 * REACH), jnp.float32)
    (grad_sum, back_sum), mixed_rows = lax.scan(per_row, (start_grad, start_back), jnp.arange(NLAT, dtype=jnp.int32))
    output = jnp.transpose(mixed_rows, (1, 0, 2))
    inner_rows = back_sum[:, 1:NLAT + 1, :]
    core_cols = inner_rows[:, :, REACH:REACH + NLON]
    core_cols = core_cols + jnp.pad(inner_rows[:, :, REACH + NLON:], ((0, 0), (0, 0), (0, NLON - REACH)))
    core_cols = core_cols + jnp.pad(inner_rows[:, :, :REACH], ((0, 0), (0, 0), (NLON - REACH, 0)))
    input_grad = core_cols.astype(jnp.bfloat16)
    weight_grad = (grad_sum * (1.0 / math.sqrt(NLAT * NLON))).reshape(-1)
    return (output, input_grad, weight_grad)
```

```python
import math

import jax
import jax.numpy as jnp
from jax import lax
from jax.experimental import pallas as pl
from jax.experimental.pallas import tpu as pltpu
from jax.sharding import PartitionSpec as P

MESH = pl.DeviceIdType.MESH
BF = jnp.bfloat16
F32 = jnp.float32

CH = 256
KB = 9
JC = 90
JP = 96
HALO = 64
NLAT_AX = 32
NLON_AX = 16
NX, NZ, NY = 4, 8, 8


def iota(shape, dim):
    return lax.broadcasted_iota(jnp.int32, shape, dim)


def onehot(cond):
    return jnp.where(cond, 1.0, 0.0).astype(BF)


def mm(a, b):
    return jnp.dot(a, b, preferred_element_type=F32)


def mm_nt(a, b):
    return lax.dot_general(a, b, (((1,), (1,)), ((), ())), preferred_element_type=F32)


def kernel(
    f_hbm, basis_hbm, hw_ref, w_hbm, c_hbm,
    out_ref, ig_ref, wg_ref,
    fv, cv, bv, wv,
    f_l, f_r, c_l, c_r,
    xf, xc,
    base_f, base_b, band_f, band_b, masks,
    pb, sb, cot_t,
    g_own, c_send, c_recv,
    x_own, x_send, x_recv,
    z_f32, z_send, z_recv,
    y_f32, y_send, y_recv,
    in_sem, lon_ss, lon_rs, lat_ss, lat_rs, c_ss, c_rs, x_ss, x_rs, z_ss, z_rs, y_ss, y_rs,
):
    lat = lax.axis_index("lat")
    lon = lax.axis_index("lon")
    core = lat % 2
    zl = (lat // 2) % 4
    x = lat // 8
    zh = lon // 8
    y = lon % 8
    z = zh * 4 + zl
    i0 = lat * 2

    def dev_x(s):
        return (((x + s) % NX) * 8 + zl * 2 + core, lon)

    def dev_z(s):
        t = (z + s) % NZ
        return (x * 8 + (t % 4) * 2 + core, (t // 4) * 8 + y)

    def dev_y(s):
        return (lat, zh * 8 + (y + s) % NY)

    dev_core = (x * 8 + zl * 2 + (1 - core), lon)
    lon_up = (lat, (lon + 1) % NLON_AX)
    lon_dn = (lat, (lon + NLON_AX - 1) % NLON_AX)
    lat_up = ((lat + 1) % NLAT_AX, lon)
    lat_dn = ((lat + NLAT_AX - 1) % NLAT_AX, lon)

    loads = [
        pltpu.make_async_copy(src, dst, in_sem.at[n])
        for n, (src, dst) in enumerate(((f_hbm, fv), (c_hbm, cv), (basis_hbm, bv), (w_hbm, wv)))
    ]
    for load in loads:
        load.start()

    barrier = pltpu.get_barrier_semaphore()
    peers = [lon_up, lon_dn, lat_up, lat_dn, dev_core]
    peers += [dev_x(s) for s in range(1, NX)]
    peers += [dev_z(s) for s in range(1, NZ)]
    peers += [dev_y(s) for s in range(1, NY)]
    for peer in peers:
        pl.semaphore_signal(barrier, inc=1, device_id=peer, device_id_type=MESH)
    pl.semaphore_wait(barrier, len(peers))

    def remote(src, dst, ss, rs, dev):
        return pltpu.make_async_remote_copy(
            src_ref=src, dst_ref=dst, send_sem=ss, recv_sem=rs, device_id=dev, device_id_type=MESH
        )

    lon_copies = []
    for n, (src, left, right) in enumerate(((f_hbm, f_l, f_r), (c_hbm, c_l, c_r))):
        lon_copies.append(
            (
                remote(src.at[pl.ds(JC - HALO, HALO)], left, lon_ss.at[2 * n], lon_rs.at[2 * n], lon_up),
                remote(src.at[pl.ds(0, HALO)], right, lon_ss.at[2 * n + 1], lon_rs.at[2 * n + 1], lon_dn),
            )
        )
    for copy in lon_copies[0] + lon_copies[1]:
        copy.start()

    p192 = iota((192, 180), 0)
    r192 = (p192 >= JP).astype(jnp.int32)
    split_own = onehot(iota((192, 180), 1) == 2 * (p192 - JP * r192) + r192)
    p128 = iota((128, 128), 0)
    r128 = (p128 >= HALO).astype(jnp.int32)
    split_halo = onehot(iota((128, 128), 1) == 2 * (p128 - HALO * r128) + r128)
    q192 = iota((180, 192), 1)
    s192 = (q192 >= JP).astype(jnp.int32)
    join_own = onehot(iota((180, 192), 0) == 2 * (q192 - JP * s192) + s192)

    def lat_copies(n, buf):
        copies = []
        for m, piece in enumerate((pl.ds(0, JP), pl.ds(128, 128))):
            q = 4 * n + 2 * m
            copies.append(
                (
                    remote(buf.at[2, piece], buf.at[0, piece], lat_ss.at[q], lat_rs.at[q], lat_up),
                    remote(buf.at[1, piece], buf.at[3, piece], lat_ss.at[q + 1], lat_rs.at[q + 1], lat_dn),
                )
            )
        return copies

    def place_own(raw, buf):
        rows = mm(split_own, raw[...].reshape(180, CH)).astype(BF)
        buf[1, 0:JP, :] = rows[0:JP]
        buf[2, 0:JP, :] = rows[JP:192]
        for row in range(4):
            buf[row, JP:128, :] = jnp.zeros((128 - JP, CH), BF)

    def place_halo(left, right, buf):
        for raw, at in ((left, 128), (right, 192)):
            rows = mm(split_halo, raw[...].reshape(128, CH)).astype(BF)
            buf[1, at : at + HALO, :] = rows[0:HALO]
            buf[2, at : at + HALO, :] = rows[HALO:128]

    lat_f = lat_copies(0, xf)
    lat_c = lat_copies(1, xc)
    loads[0].wait()
    place_own(fv, xf)
    for copy in lat_f[0]:
        copy.start()
    loads[1].wait()
    place_own(cv, xc)
    for copy in lat_c[0]:
        copy.start()

    loads[2].wait()
    n_row = iota((64, 1), 0)
    r_row = (n_row >= 27).astype(jnp.int32)
    m_row = n_row - 27 * r_row
    d_row = (m_row >= 9).astype(jnp.int32) + (m_row >= 18).astype(jnp.int32)
    k_row = m_row - 9 * d_row
    col = iota((64, 27 * 64), 1)
    lane64 = iota((64, 128), 1)
    step = r_row + d_row
    row_of = i0 + step - 1
    outside = (row_of < 0) | (row_of > 63)
    target = (d_row * 9 + k_row) * 64 + i0 + r_row
    target = jnp.where(outside, -1, target)
    taps = mm(onehot(col == target), bv[...])
    width = jnp.where(r_row == 0, hw_ref[i0], hw_ref[i0 + 1])
    base_f[...] = jnp.where(jnp.abs(lane64 - HALO) <= width, taps, 0.0)
    target = ((2 - d_row) * 9 + k_row) * 64 + row_of
    target = jnp.where(outside, -1, target)
    taps = mm(onehot(col == target), bv[...])
    widths = [hw_ref[(i0 + 63 + s) % 64] for s in range(4)]
    width = jnp.where(
        step == 0, widths[0], jnp.where(step == 1, widths[1], jnp.where(step == 2, widths[2], widths[3]))
    )
    taps = jnp.where(jnp.abs(lane64 - HALO) <= width, taps, 0.0).astype(BF)
    turn = onehot((iota((128, 128), 0) + iota((128, 128), 1)) % 128 == 0)
    base_b[...] = mm(taps, turn)

    jj = iota((JP, 128), 0)
    ll = iota((JP, 128), 1)
    for low in range(2):
        idx = 64 + ll - jj
        masks[3 * low] = onehot((idx >= low) & (idx <= 127 + low))
        masks[3 * low + 1] = onehot((ll < HALO) & (ll - jj >= low))
        masks[3 * low + 2] = onehot((ll >= HALO) & (JC + ll - jj <= 127 + low))

    def build(base, band, low):
        def body(k, carry):
            at = pl.multiple_of(k * JP, JP)
            for r in range(2):
                for d in range(3):
                    row = base[pl.ds((r * 3 + d) * 9 + k, 1), :].astype(BF)
                    wide = jnp.broadcast_to(row, (JP, 128))
                    s0 = pltpu.roll(wide, 0, 1, stride=1, stride_axis=0)
                    s1 = pltpu.roll(s0, 64, 1)
                    s2 = pltpu.roll(s0, 38, 1)
                    band[r, pl.ds(at, JP), d * 256 : d * 256 + 128] = s1 * masks[3 * low]
                    band[r, pl.ds(at, JP), d * 256 + 128 : d * 256 + 256] = (
                        s0 * masks[3 * low + 1] + s2 * masks[3 * low + 2]
                    )
            return carry

        lax.fori_loop(0, KB, body, 0)

    for copy in lon_copies[0]:
        copy.wait_recv()
    place_halo(f_l, f_r, xf)
    for copy in lat_f[1]:
        copy.start()

    build(base_f, band_f, 0)

    o_new = iota((256, 1), 0)
    mine = (o_new >= 128).astype(jnp.int32)
    o_in = o_new - 128 * mine
    sx = (o_in // 32 + x) % NX
    sz = ((o_in % 32) // 4 + z) % NZ
    bit = mine * core + (1 - mine) * (1 - core)
    o_old = sx * 64 + (sz % 4) * 16 + bit * 8 + (sz // 4) * 4 + o_in % 4
    order = onehot(iota((256, 256), 1) == o_old)
    cot_rows = jnp.concatenate([xc[1, 0:JP, :], xc[2, 0:JP, :]], axis=0)
    cot_t[...] = mm_nt(order, cot_rows).astype(BF)

    def conv(band, buf, dst):
        for r in range(2):
            res = mm(band[r], buf[r : r + 3].reshape(768, CH)).astype(BF)
            for k in range(KB):
                dst[k, r * JP : (r + 1) * JP, :] = res[k * JP : (k + 1) * JP]

    for pair in lat_f:
        for copy in pair:
            copy.wait_recv()
    conv(band_f, xf, pb)

    def core_copy(k):
        return remote(c_send.at[k], c_recv.at[k], c_ss.at[k], c_rs.at[k], dev_core)

    def grad_body(k, carry):
        g = mm(cot_t[...], pb[k])
        c_send[k] = g[0:128].astype(BF)
        core_copy(k).start()
        g_own[k] = g[128:256]
        return carry

    lax.fori_loop(0, KB, grad_body, 0)

    for copy in lon_copies[1]:
        copy.wait_recv()
    place_halo(c_l, c_r, xc)
    for copy in lat_c[1]:
        copy.start()

    def x_copy(s, g):
        return remote(
            x_send.at[s - 1, pl.ds(3 * g, 3)],
            x_recv.at[s - 1, pl.ds(3 * g, 3)],
            x_ss.at[s - 1, g],
            x_rs.at[s - 1, g],
            dev_x(s),
        )

    for g in range(3):
        for k in range(3 * g, 3 * g + 3):
            core_copy(k).wait_recv()
            total = g_own[k] + c_recv[k].astype(F32)
            x_own[k] = total[0:32]
            for s in range(1, NX):
                x_send[s - 1, k] = total[32 * s : 32 * s + 32].astype(BF)
        for s in range(1, NX):
            x_copy(s, g).start()

    loads[3].wait()
    mixed = mm_nt(pb[0], wv[0])
    for k in range(1, KB):
        mixed = mixed + mm_nt(pb[k], wv[k])
    out_ref[...] = mm(join_own, mixed.astype(BF)).astype(BF).reshape(JC, 2, CH)

    build(base_b, band_b, 1)
    for pair in lat_c:
        for copy in pair:
            copy.wait_recv()
    conv(band_b, xc, sb)
    grad = mm(sb[0], wv[0])
    for k in range(1, KB):
        grad = grad + mm(sb[k], wv[k])
    ig_ref[...] = mm(join_own, grad.astype(BF)).astype(BF).reshape(JC, 2, CH)

    for g in range(3):
        for s in range(1, NX):
            x_copy(s, g).wait_recv()
        for k in range(3 * g, 3 * g + 3):
            total = x_own[k]
            for s in range(1, NX):
                total = total + x_recv[s - 1, k].astype(F32)
            for h in range(2):
                z_f32[pl.ds(2 * k + h, 32, stride=18), :] = total[:, 128 * h : 128 * h + 128]

    def z_copy(s):
        return remote(z_send.at[s - 1], z_recv.at[s - 1], z_ss.at[s - 1], z_rs.at[s - 1], dev_z(s))

    for s in range(1, NZ):
        z_send[s - 1, 0:72, :] = z_f32[72 * s : 72 * s + 72, :].astype(BF)
        z_send[s - 1, 72:80, :] = jnp.zeros((8, 128), BF)
        z_copy(s).start()
    total = z_f32[0:72, :]
    for s in range(1, NZ):
        z_copy(s).wait_recv()
        total = total + z_recv[s - 1, 0:72, :].astype(F32)
    y_f32[...] = total

    def y_copy(s):
        return remote(y_send.at[s - 1], y_recv.at[s - 1], y_ss.at[s - 1], y_rs.at[s - 1], dev_y(s))

    for s in range(1, NY):
        rows = y_f32[pl.ds(9 * ((y + s) % NY), 9), :]
        y_send[s - 1] = jnp.concatenate([rows, jnp.zeros((7, 128), F32)], axis=0).astype(BF)
        y_copy(s).start()
    total = y_f32[pl.ds(9 * y, 9), :]
    for s in range(1, NY):
        y_copy(s).wait_recv()
        total = total + y_recv[s - 1].astype(F32)[0:9]
    wg_ref[...] = total * (1.0 / math.sqrt(2 * NLAT_AX * JC * NLON_AX))

    for pair in lon_copies + lat_f + lat_c:
        for copy in pair:
            copy.wait_send()
    for k in range(KB):
        core_copy(k).wait_send()
    for g in range(3):
        for s in range(1, NX):
            x_copy(s, g).wait_send()
    for s in range(1, NZ):
        z_copy(s).wait_send()
    for s in range(1, NY):
        y_copy(s).wait_send()


def local(fields, basis, half_width, weight, cotangent):
    dma = pltpu.SemaphoreType.DMA
    vmem = pltpu.VMEM
    any_spec = pl.BlockSpec(memory_space=pl.ANY)
    vm_spec = pl.BlockSpec(memory_space=pltpu.VMEM)
    out, ig, wg = pl.pallas_call(
        kernel,
        out_shape=(
            jax.ShapeDtypeStruct((JC, 2, CH), BF),
            jax.ShapeDtypeStruct((JC, 2, CH), BF),
            jax.ShapeDtypeStruct((9, 128), F32),
        ),
        in_specs=[any_spec, any_spec, pl.BlockSpec(memory_space=pltpu.SMEM), any_spec, any_spec],
        out_specs=(vm_spec, vm_spec, vm_spec),
        scratch_shapes=[
            vmem((JC, 2, CH), BF), vmem((JC, 2, CH), BF), vmem((27 * 64, 128), BF), vmem((KB, CH, CH), BF),
            vmem((HALO, 2, CH), BF), vmem((HALO, 2, CH), BF), vmem((HALO, 2, CH), BF), vmem((HALO, 2, CH), BF),
            vmem((4, 256, CH), BF), vmem((4, 256, CH), BF),
            vmem((64, 128), F32), vmem((64, 128), F32),
            vmem((2, KB * JP, 768), BF), vmem((2, KB * JP, 768), BF), vmem((6, JP, 128), BF),
            vmem((KB, 2 * JP, CH), BF), vmem((KB, 2 * JP, CH), BF), vmem((CH, 2 * JP), BF),
            vmem((KB, 128, CH), F32), vmem((KB, 128, CH), BF), vmem((KB, 128, CH), BF),
            vmem((KB, 32, CH), F32), vmem((3, KB, 32, CH), BF), vmem((3, KB, 32, CH), BF),
            vmem((32 * 18, 128), F32), vmem((7, 80, 128), BF), vmem((7, 80, 128), BF),
            vmem((72, 128), F32), vmem((7, 16, 128), BF), vmem((7, 16, 128), BF),
            dma((4,)), dma((4,)), dma((4,)), dma((8,)), dma((8,)), dma((KB,)), dma((KB,)),
            dma((3, 3)), dma((3, 3)), dma((7,)), dma((7,)), dma((7,)), dma((7,)),
        ],
        compiler_params=pltpu.CompilerParams(
            collective_id=0, has_side_effects=True, vmem_limit_bytes=48 * 1024 * 1024
        ),
    )(
        jnp.transpose(fields, (2, 1, 0)),
        jnp.transpose(basis, (1, 2, 0, 3)).reshape(27 * 64, 128),
        half_width,
        jnp.transpose(weight, (1, 0, 2)),
        jnp.transpose(cotangent, (2, 1, 0)),
    )
    return jnp.transpose(out, (2, 1, 0)), jnp.transpose(ig, (2, 1, 0)), wg.reshape(-1)


def solution(mesh):
    placed = (P(None, "lat", "lon"), P(), P(), P(), P(None, "lat", "lon"))
    return jax.shard_map(
        local,
        mesh=mesh,
        in_specs=placed,
        out_specs=(P(None, "lat", "lon"), P(None, "lat", "lon"), P(("lat", "lon"))),
        check_vma=False,
    )
```

```python
import math

import jax
import jax.numpy as jnp
from jax import lax
from jax.experimental import pallas as pl
from jax.experimental.pallas import tpu as pltpu
from jax.sharding import PartitionSpec as P

MESH = pl.DeviceIdType.MESH
BF = jnp.bfloat16
F32 = jnp.float32

CH = 256
KB = 9
JC = 90
JP = 96
HALO = 64
NLAT_AX = 32
NLON_AX = 16
NX, NZ, NY = 4, 8, 8


def iota(shape, dim):
    return lax.broadcasted_iota(jnp.int32, shape, dim)


def onehot(cond):
    return jnp.where(cond, 1.0, 0.0).astype(BF)


def mm(a, b):
    return jnp.dot(a, b, preferred_element_type=F32)


def mm_nt(a, b):
    return lax.dot_general(a, b, (((1,), (1,)), ((), ())), preferred_element_type=F32)


def kernel(
    f_hbm, basis_hbm, hw_hbm, w_hbm, c_hbm,
    out_ref, ig_ref, wg_ref,
    fv, cv, bv, hw_ref, wv,
    f_last, c_last,
    xf, xc,
    base_f, base_b, band_f, band_b, masks,
    pb, sb, cot_t,
    g_own, c_send, c_recv,
    xa_own, xa_send, xa_recv,
    zb_own, zb_send, zb_recv,
    za_f32, za_send, za_recv,
    xb_f32, xb_send, xb_recv,
    ya_f32, yb_f32, y_send, y_recv,
    in_sem, halo_ss, halo_rs, c_ss, c_rs, xa_ss, xa_rs, zb_ss, zb_rs, za_ss, za_rs, xb_ss, xb_rs, y_ss, y_rs,
):
    lat = lax.axis_index("lat")
    lon = lax.axis_index("lon")
    core = lat % 2
    zl = (lat // 2) % 4
    x = lat // 8
    zh = lon // 8
    y = lon % 8
    z = zh * 4 + zl
    i0 = lat * 2

    def dev_x(s):
        return (((x + s) % NX) * 8 + zl * 2 + core, lon)

    def dev_z(s):
        t = (z + s) % NZ
        return (x * 8 + (t % 4) * 2 + core, (t // 4) * 8 + y)

    def dev_y(s):
        return (lat, zh * 8 + (y + s) % NY)

    dev_core = (x * 8 + zl * 2 + (1 - core), lon)

    def near(up, right):
        return ((lat + NLAT_AX + up) % NLAT_AX, (lon + NLON_AX + right) % NLON_AX)

    barrier = pltpu.get_barrier_semaphore()
    peers = [near(u, r) for u in (-1, 0, 1) for r in (-1, 0, 1) if u or r]
    peers += [dev_core]
    peers += [dev_x(s) for s in range(1, NX)]
    peers += [dev_z(s) for s in range(1, NZ)]
    peers += [dev_y(s) for s in range(1, NY)]
    for peer in peers:
        pl.semaphore_signal(barrier, inc=1, device_id=peer, device_id_type=MESH)

    loads = [
        pltpu.make_async_copy(src, dst, in_sem.at[n])
        for n, (src, dst) in enumerate(
            ((f_hbm, fv), (c_hbm, cv), (basis_hbm, bv), (hw_hbm, hw_ref), (w_hbm, wv))
        )
    ]
    for load in loads:
        load.start()

    def remote(src, dst, ss, rs, dev):
        return pltpu.make_async_remote_copy(
            src_ref=src, dst_ref=dst, send_sem=ss, recv_sem=rs, device_id=dev, device_id_type=MESH
        )

    p = iota((320, 180), 0)
    r_own = (p >= JP).astype(jnp.int32)
    r_last = (p >= 256).astype(jnp.int32)
    want = jnp.where(p < 192, 2 * (p - JP * r_own) + r_own, 2 * (p - 192 - HALO * r_last + JC - HALO) + r_last)
    split = onehot(iota((320, 180), 1) == want)
    q192 = iota((180, 192), 1)
    s192 = (q192 >= JP).astype(jnp.int32)
    join_own = onehot(iota((180, 192), 0) == 2 * (q192 - JP * s192) + s192)

    def place(raw, buf, last):
        rows = mm(split, raw[...].reshape(180, CH)).astype(BF)
        buf[1, 0:JP, :] = rows[0:JP]
        buf[2, 0:JP, :] = rows[JP:192]
        last[0] = rows[192:256]
        last[1] = rows[256:320]
        for row in range(4):
            buf[row, JP:128, :] = jnp.zeros((128 - JP, CH), BF)

    both, own, first = pl.ds(1, 2), pl.ds(0, JP), pl.ds(0, HALO)
    left, right = pl.ds(128, HALO), pl.ds(192, HALO)

    def halo_copies(n, buf, last):
        moves = (
            (last, buf.at[both, left], near(0, 1)),
            (buf.at[both, first], buf.at[both, right], near(0, -1)),
            (buf.at[2, own], buf.at[0, own], near(1, 0)),
            (buf.at[1, own], buf.at[3, own], near(-1, 0)),
            (last.at[1], buf.at[0, left], near(1, 1)),
            (buf.at[2, first], buf.at[0, right], near(1, -1)),
            (last.at[0], buf.at[3, left], near(-1, 1)),
            (buf.at[1, first], buf.at[3, right], near(-1, -1)),
        )
        return [
            remote(src, dst, halo_ss.at[8 * n + m], halo_rs.at[8 * n + m], dev)
            for m, (src, dst, dev) in enumerate(moves)
        ]

    loads[0].wait()
    place(fv, xf, f_last)
    pl.semaphore_wait(barrier, len(peers))
    halo_f = halo_copies(0, xf, f_last)
    halo_c = halo_copies(1, xc, c_last)
    for copy in halo_f:
        copy.start()
    loads[1].wait()
    place(cv, xc, c_last)

    loads[2].wait()
    loads[3].wait()
    n_row = iota((64, 1), 0)
    r_row = (n_row >= 27).astype(jnp.int32)
    m_row = n_row - 27 * r_row
    d_row = (m_row >= 9).astype(jnp.int32) + (m_row >= 18).astype(jnp.int32)
    k_row = m_row - 9 * d_row
    col = iota((64, 27 * 64), 1)
    lane64 = iota((64, 128), 1)
    step = r_row + d_row
    row_of = i0 + step - 1
    outside = (row_of < 0) | (row_of > 63)
    target = (d_row * 9 + k_row) * 64 + i0 + r_row
    target = jnp.where(outside, -1, target)
    taps = mm(onehot(col == target), bv[...])
    width = jnp.where(r_row == 0, hw_ref[i0], hw_ref[i0 + 1])
    base_f[...] = jnp.where(jnp.abs(lane64 - HALO) <= width, taps, 0.0)
    target = ((2 - d_row) * 9 + k_row) * 64 + row_of
    target = jnp.where(outside, -1, target)
    taps = mm(onehot(col == target), bv[...])
    widths = [hw_ref[(i0 + 63 + s) % 64] for s in range(4)]
    width = jnp.where(
        step == 0, widths[0], jnp.where(step == 1, widths[1], jnp.where(step == 2, widths[2], widths[3]))
    )
    taps = jnp.where(jnp.abs(lane64 - HALO) <= width, taps, 0.0).astype(BF)
    turn = onehot((iota((128, 128), 0) + iota((128, 128), 1)) % 128 == 0)
    base_b[...] = mm(taps, turn)

    jj = iota((JP, 128), 0)
    ll = iota((JP, 128), 1)
    for low in range(2):
        idx = 64 + ll - jj
        masks[3 * low] = onehot((idx >= low) & (idx <= 127 + low))
        masks[3 * low + 1] = onehot((ll < HALO) & (ll - jj >= low))
        masks[3 * low + 2] = onehot((ll >= HALO) & (JC + ll - jj <= 127 + low))

    def build(base, band, low):
        def body(k, carry):
            at = pl.multiple_of(k * JP, JP)
            for r in range(2):
                for d in range(3):
                    row = base[pl.ds((r * 3 + d) * 9 + k, 1), :].astype(BF)
                    wide = jnp.broadcast_to(row, (JP, 128))
                    s0 = pltpu.roll(wide, 0, 1, stride=1, stride_axis=0)
                    s1 = pltpu.roll(s0, 64, 1)
                    s2 = pltpu.roll(s0, 38, 1)
                    band[r, pl.ds(at, JP), d * 256 : d * 256 + 128] = s1 * masks[3 * low]
                    band[r, pl.ds(at, JP), d * 256 + 128 : d * 256 + 256] = (
                        s0 * masks[3 * low + 1] + s2 * masks[3 * low + 2]
                    )
            return carry

        lax.fori_loop(0, KB, body, 0)

    build(base_f, band_f, 0)
    for copy in halo_c:
        copy.start()

    o_new = iota((256, 1), 0)
    mine = (o_new >= 128).astype(jnp.int32)
    o_in = o_new - 128 * mine
    bit = mine * core + (1 - mine) * (1 - core)
    cot_rows = jnp.concatenate([xc[1, 0:JP, :], xc[2, 0:JP, :]], axis=0)
    for n, (dx, dz) in enumerate(((o_in // 32, (o_in % 32) // 4), ((o_in % 16) // 4, o_in // 16))):
        sx = (dx + x) % NX
        sz = (dz + z) % NZ
        o_old = sx * 64 + (sz % 4) * 16 + bit * 8 + (sz // 4) * 4 + o_in % 4
        order = onehot(iota((256, 256), 1) == o_old)
        cot_t[n] = mm_nt(order, cot_rows).astype(BF)

    build(base_b, band_b, 1)

    def conv(band, buf, dst):
        for r in range(2):
            res = mm(band[r], buf[r : r + 3].reshape(768, CH)).astype(BF)
            for k in range(KB):
                dst[k, r * JP : (r + 1) * JP, :] = res[k * JP : (k + 1) * JP]

    for copy in halo_f:
        copy.wait_recv()
    conv(band_f, xf, pb)

    def core_copy(k):
        return remote(c_send.at[k], c_recv.at[k], c_ss.at[k], c_rs.at[k], dev_core)

    for g in range(3):

        def grad_body(k, carry, order=g % 2):
            part = mm(cot_t[order], pb[k])
            c_send[k] = part[0:128].astype(BF)
            core_copy(k).start()
            g_own[k] = part[128:256]
            return carry

        lax.fori_loop(3 * g, 3 * g + 3, grad_body, 0)

    def xa_copy(s, g):
        part = pl.ds(3 * g, 3)
        return remote(
            xa_send.at[s - 1, part], xa_recv.at[s - 1, part], xa_ss.at[s - 1, g], xa_rs.at[s - 1, g], dev_x(s)
        )

    def zb_copy(s):
        return remote(zb_send.at[s - 1], zb_recv.at[s - 1], zb_ss.at[s - 1], zb_rs.at[s - 1], dev_z(s))

    for g in range(3):
        for m in range(3):
            k = 3 * g + m
            core_copy(k).wait_recv()
            total = g_own[k] + c_recv[k].astype(F32)
            if g == 1:
                zb_own[m] = total[0:16]
                for s in range(1, NZ):
                    zb_send[s - 1, m] = total[16 * s : 16 * s + 16].astype(BF)
            else:
                at = 3 * (g // 2) + m
                xa_own[at] = total[0:32]
                for s in range(1, NX):
                    xa_send[s - 1, at] = total[32 * s : 32 * s + 32].astype(BF)
        if g == 1:
            for s in range(1, NZ):
                zb_copy(s).start()
        else:
            for s in range(1, NX):
                xa_copy(s, g // 2).start()

    loads[4].wait()
    mixed = mm_nt(pb[0], wv[0])
    for k in range(1, KB):
        mixed = mixed + mm_nt(pb[k], wv[k])
    out_ref[...] = mm(join_own, mixed.astype(BF)).astype(BF).reshape(JC, 2, CH)

    for copy in halo_c:
        copy.wait_recv()
    conv(band_b, xc, sb)
    grad = mm(sb[0], wv[0])
    for k in range(1, KB):
        grad = grad + mm(sb[k], wv[k])
    ig_ref[...] = mm(join_own, grad.astype(BF)).astype(BF).reshape(JC, 2, CH)

    def za_copy(s):
        return remote(za_send.at[s - 1], za_recv.at[s - 1], za_ss.at[s - 1], za_rs.at[s - 1], dev_z(s))

    def xb_copy(s):
        return remote(xb_send.at[s - 1], xb_recv.at[s - 1], xb_ss.at[s - 1], xb_rs.at[s - 1], dev_x(s))

    for g in range(2):
        for s in range(1, NX):
            xa_copy(s, g).wait_recv()
        for at in range(3 * g, 3 * g + 3):
            total = xa_own[at]
            for s in range(1, NX):
                total = total + xa_recv[s - 1, at].astype(F32)
            for h in range(2):
                za_f32[pl.ds(2 * at + h, 32, stride=12), :] = total[:, 128 * h : 128 * h + 128]
    for s in range(1, NZ):
        za_send[s - 1] = za_f32[48 * s : 48 * s + 48, :].astype(BF)
        za_copy(s).start()
    for s in range(1, NZ):
        zb_copy(s).wait_recv()
    for m in range(3):
        total = zb_own[m]
        for s in range(1, NZ):
            total = total + zb_recv[s - 1, m].astype(F32)
        for h in range(2):
            xb_f32[pl.ds(2 * m + h, 16, stride=6), :] = total[:, 128 * h : 128 * h + 128]
    for s in range(1, NX):
        xb_send[s - 1, 0:24, :] = xb_f32[24 * s : 24 * s + 24, :].astype(BF)
        xb_send[s - 1, 24:32, :] = jnp.zeros((8, 128), BF)
        xb_copy(s).start()

    def y_copy(s):
        return remote(y_send.at[s - 1], y_recv.at[s - 1], y_ss.at[s - 1], y_rs.at[s - 1], dev_y(s))

    total = xb_f32[0:24, :]
    for s in range(1, NX):
        xb_copy(s).wait_recv()
        total = total + xb_recv[s - 1, 0:24, :].astype(F32)
    yb_f32[...] = total
    total = za_f32[0:48, :]
    for s in range(1, NZ):
        za_copy(s).wait_recv()
        total = total + za_recv[s - 1].astype(F32)
    ya_f32[...] = total

    def y_rows(to):
        return [ya_f32[pl.ds(6 * to, 6), :], yb_f32[pl.ds(3 * to, 3), :]]

    for s in range(1, NY):
        rows = y_rows((y + s) % NY)
        y_send[s - 1] = jnp.concatenate(rows + [jnp.zeros((7, 128), F32)], axis=0).astype(BF)
        y_copy(s).start()
    total = jnp.concatenate(y_rows(y), axis=0)
    for s in range(1, NY):
        y_copy(s).wait_recv()
        total = total + y_recv[s - 1].astype(F32)[0:9]
    total = jnp.where(y % 2 == 0, total, jnp.concatenate([total[6:9], total[0:6]], axis=0))
    wg_ref[...] = total * (1.0 / math.sqrt(2 * NLAT_AX * JC * NLON_AX))

    for copy in halo_f + halo_c:
        copy.wait_send()
    for k in range(KB):
        core_copy(k).wait_send()
    for s in range(1, NX):
        xa_copy(s, 0).wait_send()
        xa_copy(s, 1).wait_send()
        xb_copy(s).wait_send()
    for s in range(1, NZ):
        zb_copy(s).wait_send()
        za_copy(s).wait_send()
    for s in range(1, NY):
        y_copy(s).wait_send()


def local(fields, basis, half_width, weight, cotangent):
    dma = pltpu.SemaphoreType.DMA
    vmem = pltpu.VMEM
    hbm_spec = pl.BlockSpec(memory_space=pltpu.HBM)
    vm_spec = pl.BlockSpec(memory_space=pltpu.VMEM)
    shapes = (
        jax.ShapeDtypeStruct((JC, 2, CH), BF),
        jax.ShapeDtypeStruct((JC, 2, CH), BF),
        jax.ShapeDtypeStruct((9, 128), F32),
    )
    results = pl.pallas_call(
        kernel,
        out_shape=shapes,
        in_specs=[hbm_spec] * 5,
        out_specs=(vm_spec,) * 3,
        scratch_shapes=[
            vmem((JC, 2, CH), BF), vmem((JC, 2, CH), BF), vmem((27 * 64, 128), BF),
            pltpu.SMEM((64,), jnp.int32), vmem((KB, CH, CH), BF),
            vmem((2, HALO, CH), BF), vmem((2, HALO, CH), BF),
            vmem((4, 256, CH), BF), vmem((4, 256, CH), BF),
            vmem((64, 128), F32), vmem((64, 128), F32),
            vmem((2, KB * JP, 768), BF), vmem((2, KB * JP, 768), BF), vmem((6, JP, 128), BF),
            vmem((KB, 2 * JP, CH), BF), vmem((KB, 2 * JP, CH), BF), vmem((2, CH, 2 * JP), BF),
            vmem((KB, 128, CH), F32), vmem((KB, 128, CH), BF), vmem((KB, 128, CH), BF),
            vmem((6, 32, CH), F32), vmem((3, 6, 32, CH), BF), vmem((3, 6, 32, CH), BF),
            vmem((3, 16, CH), F32), vmem((7, 3, 16, CH), BF), vmem((7, 3, 16, CH), BF),
            vmem((32 * 12, 128), F32), vmem((7, 48, 128), BF), vmem((7, 48, 128), BF),
            vmem((16 * 6, 128), F32), vmem((3, 32, 128), BF), vmem((3, 32, 128), BF),
            vmem((48, 128), F32), vmem((24, 128), F32), vmem((7, 16, 128), BF), vmem((7, 16, 128), BF),
            dma((5,)), dma((16,)), dma((16,)), dma((KB,)), dma((KB,)), dma((3, 2)), dma((3, 2)),
            dma((7,)), dma((7,)), dma((7,)), dma((7,)), dma((3,)), dma((3,)), dma((7,)), dma((7,)),
        ],
        compiler_params=pltpu.CompilerParams(
            collective_id=0, has_side_effects=True, vmem_limit_bytes=48 * 1024 * 1024
        ),
    )(
        *[
            pltpu.with_memory_space_constraint(a, pltpu.HBM)
            for a in (
                jnp.transpose(fields, (2, 1, 0)),
                jnp.transpose(basis, (1, 2, 0, 3)).reshape(27 * 64, 128),
                half_width,
                jnp.transpose(weight, (1, 0, 2)),
                jnp.transpose(cotangent, (2, 1, 0)),
            )
        ]
    )
    out, ig, wg = results
    return jnp.transpose(out, (2, 1, 0)), jnp.transpose(ig, (2, 1, 0)), wg.reshape(-1)


def solution(mesh):
    placed = (P(None, "lat", "lon"), P(), P(), P(), P(None, "lat", "lon"))
    return jax.shard_map(
        local,
        mesh=mesh,
        in_specs=placed,
        out_specs=(P(None, "lat", "lon"), P(None, "lat", "lon"), P(("lat", "lon"))),
        check_vma=False,
    )
```

```python
import math

import jax
import jax.numpy as jnp
from jax import lax
from jax.experimental import pallas as pl
from jax.experimental.pallas import tpu as pltpu
from jax.sharding import PartitionSpec as P

MESH = pl.DeviceIdType.MESH
BF = jnp.bfloat16
F32 = jnp.float32

CH = 256
KB = 9
JC = 90
JP = 96
HALO = 64
NLAT_AX = 32
NLON_AX = 16
NX, NZ, NY = 4, 8, 8
FAR4 = (2, 1, 3)
FAR8 = (4, 3, 5, 2, 6, 1, 7)
NEAR4 = FAR4[::-1]
NEAR8 = FAR8[::-1]


def iota(shape, dim):
    return lax.broadcasted_iota(jnp.int32, shape, dim)


def onehot(cond):
    return jnp.where(cond, 1.0, 0.0).astype(BF)


def mm(a, b):
    return jnp.dot(a, b, preferred_element_type=F32)


def mm_nt(a, b):
    return lax.dot_general(a, b, (((1,), (1,)), ((), ())), preferred_element_type=F32)


def kernel(
    f_hbm, basis_hbm, hw_hbm, w_hbm, c_hbm,
    both_ref, wg_ref,
    fv, cv, bv, hw_ref, wv,
    f_last, c_last,
    xf, xc,
    base_f, base_b, band_f, band_b, masks,
    pb, sb, cot_t,
    g_own, c_send, c_recv,
    xa_own, xa_send, xa_recv,
    zb_own, zb_send, zb_recv,
    za_f32, za_send, za_recv,
    xb_f32, xb_send, xb_recv,
    ya_f32, yb_f32, y_send, y_recv,
    in_sem, halo_ss, halo_rs, c_ss, c_rs, xa_ss, xa_rs, zb_ss, zb_rs, za_ss, za_rs, xb_ss, xb_rs, y_ss, y_rs,
):
    lat = lax.axis_index("lat")
    lon = lax.axis_index("lon")
    core = lat % 2
    zl = (lat // 2) % 4
    x = lat // 8
    zh = lon // 8
    y = lon % 8
    z = zh * 4 + zl
    i0 = lat * 2

    def dev_x(s):
        return (((x + s) % NX) * 8 + zl * 2 + core, lon)

    def dev_z(s):
        t = (z + s) % NZ
        return (x * 8 + (t % 4) * 2 + core, (t // 4) * 8 + y)

    def dev_y(s):
        return (lat, zh * 8 + (y + s) % NY)

    dev_core = (x * 8 + zl * 2 + (1 - core), lon)

    def near(up, right):
        return ((lat + NLAT_AX + up) % NLAT_AX, (lon + NLON_AX + right) % NLON_AX)

    barrier = pltpu.get_barrier_semaphore()
    peers = [near(u, r) for u in (-1, 0, 1) for r in (-1, 0, 1) if u or r]
    peers += [dev_core]
    peers += [dev_x(s) for s in range(1, NX)]
    peers += [dev_z(s) for s in range(1, NZ)]
    peers += [dev_y(s) for s in range(1, NY)]
    for peer in peers:
        pl.semaphore_signal(barrier, inc=1, device_id=peer, device_id_type=MESH)

    loads = [
        pltpu.make_async_copy(src, dst, in_sem.at[n])
        for n, (src, dst) in enumerate(
            ((f_hbm, fv), (c_hbm, cv), (basis_hbm, bv), (hw_hbm, hw_ref), (w_hbm, wv))
        )
    ]
    for load in loads:
        load.start()

    def remote(src, dst, ss, rs, dev):
        return pltpu.make_async_remote_copy(
            src_ref=src, dst_ref=dst, send_sem=ss, recv_sem=rs, device_id=dev, device_id_type=MESH
        )

    p = iota((320, 180), 0)
    r_own = (p >= JP).astype(jnp.int32)
    r_last = (p >= 256).astype(jnp.int32)
    want = jnp.where(p < 192, 2 * (p - JP * r_own) + r_own, 2 * (p - 192 - HALO * r_last + JC - HALO) + r_last)
    split = onehot(iota((320, 180), 1) == want)
    q192 = iota((180, 192), 1)
    s192 = (q192 >= JP).astype(jnp.int32)
    join_own = onehot(iota((180, 192), 0) == 2 * (q192 - JP * s192) + s192)

    def place(raw, buf, last):
        rows = mm(split, raw[...].reshape(180, CH)).astype(BF)
        buf[1, 0:JP, :] = rows[0:JP]
        buf[2, 0:JP, :] = rows[JP:192]
        last[0] = rows[192:256]
        last[1] = rows[256:320]
        for row in range(4):
            buf[row, JP:128, :] = jnp.zeros((128 - JP, CH), BF)

    both, own, first = pl.ds(1, 2), pl.ds(0, JP), pl.ds(0, HALO)
    left, right, sides = pl.ds(128, HALO), pl.ds(192, HALO), pl.ds(128, 2 * HALO)

    def halo_copies(n, buf, last):
        moves = (
            (last, buf.at[both, left], near(0, 1)),
            (buf.at[both, first], buf.at[both, right], near(0, -1)),
            (buf.at[2, own], buf.at[0, own], near(1, 0)),
            (buf.at[1, own], buf.at[3, own], near(-1, 0)),
        )
        if n == 0:
            moves += (
                (last.at[1], buf.at[0, left], near(1, 1)),
                (buf.at[2, first], buf.at[0, right], near(1, -1)),
                (last.at[0], buf.at[3, left], near(-1, 1)),
                (buf.at[1, first], buf.at[3, right], near(-1, -1)),
            )
        else:
            moves += (
                (buf.at[2, sides], buf.at[0, sides], near(1, 0)),
                (buf.at[1, sides], buf.at[3, sides], near(-1, 0)),
            )
        return [
            remote(src, dst, halo_ss.at[8 * n + m], halo_rs.at[8 * n + m], dev)
            for m, (src, dst, dev) in enumerate(moves)
        ]

    loads[0].wait()
    place(fv, xf, f_last)
    pl.semaphore_wait(barrier, len(peers))
    halo_f = halo_copies(0, xf, f_last)
    halo_c = halo_copies(1, xc, c_last)
    for copy in halo_f:
        copy.start()
    loads[1].wait()
    place(cv, xc, c_last)

    loads[2].wait()
    loads[3].wait()
    n_row = iota((64, 1), 0)
    r_row = (n_row >= 27).astype(jnp.int32)
    m_row = n_row - 27 * r_row
    d_row = (m_row >= 9).astype(jnp.int32) + (m_row >= 18).astype(jnp.int32)
    k_row = m_row - 9 * d_row
    col = iota((64, 27 * 64), 1)
    lane64 = iota((64, 128), 1)
    step = r_row + d_row
    row_of = i0 + step - 1
    outside = (row_of < 0) | (row_of > 63)
    target = (d_row * 9 + k_row) * 64 + i0 + r_row
    target = jnp.where(outside, -1, target)
    taps = mm(onehot(col == target), bv[...])
    width = jnp.where(r_row == 0, hw_ref[i0], hw_ref[i0 + 1])
    base_f[...] = jnp.where(jnp.abs(lane64 - HALO) <= width, taps, 0.0)
    target = ((2 - d_row) * 9 + k_row) * 64 + row_of
    target = jnp.where(outside, -1, target)
    taps = mm(onehot(col == target), bv[...])
    widths = [hw_ref[(i0 + 63 + s) % 64] for s in range(4)]
    width = jnp.where(
        step == 0, widths[0], jnp.where(step == 1, widths[1], jnp.where(step == 2, widths[2], widths[3]))
    )
    taps = jnp.where(jnp.abs(lane64 - HALO) <= width, taps, 0.0).astype(BF)
    turn = onehot((iota((128, 128), 0) + iota((128, 128), 1)) % 128 == 0)
    base_b[...] = mm(taps, turn)

    jj = iota((JP, 128), 0)
    ll = iota((JP, 128), 1)
    for low in range(2):
        idx = 64 + ll - jj
        masks[3 * low] = onehot((idx >= low) & (idx <= 127 + low))
        masks[3 * low + 1] = onehot((ll < HALO) & (ll - jj >= low))
        masks[3 * low + 2] = onehot((ll >= HALO) & (JC + ll - jj <= 127 + low))

    def build(base, band, low):
        def body(k, carry):
            at = pl.multiple_of(k * JP, JP)
            for r in range(2):
                for d in range(3):
                    row = base[pl.ds((r * 3 + d) * 9 + k, 1), :].astype(BF)
                    wide = jnp.broadcast_to(row, (JP, 128))
                    s0 = pltpu.roll(wide, 0, 1, stride=1, stride_axis=0)
                    s1 = pltpu.roll(s0, 64, 1)
                    s2 = pltpu.roll(s0, 38, 1)
                    band[r, pl.ds(at, JP), d * 256 : d * 256 + 128] = s1 * masks[3 * low]
                    band[r, pl.ds(at, JP), d * 256 + 128 : d * 256 + 256] = (
                        s0 * masks[3 * low + 1] + s2 * masks[3 * low + 2]
                    )
            return carry

        lax.fori_loop(0, KB, body, 0)

    build(base_f, band_f, 0)

    o_new = iota((256, 1), 0)
    mine = (o_new >= 128).astype(jnp.int32)
    o_in = o_new - 128 * mine
    bit = mine * core + (1 - mine) * (1 - core)
    cot_rows = jnp.concatenate([xc[1, 0:JP, :], xc[2, 0:JP, :]], axis=0)
    for n, (dx, dz) in enumerate(((o_in // 32, (o_in % 32) // 4), ((o_in % 16) // 4, o_in // 16))):
        sx = (dx + x) % NX
        sz = (dz + z) % NZ
        o_old = sx * 64 + (sz % 4) * 16 + bit * 8 + (sz // 4) * 4 + o_in % 4
        order = onehot(iota((256, 256), 1) == o_old)
        cot_t[n] = mm_nt(order, cot_rows).astype(BF)

    build(base_b, band_b, 1)

    def conv(band, buf, dst):
        for r in range(2):
            res = mm(band[r], buf[r : r + 3].reshape(768, CH)).astype(BF)
            for k in range(KB):
                dst[k, r * JP : (r + 1) * JP, :] = res[k * JP : (k + 1) * JP]

    for copy in halo_f:
        copy.wait_recv()
    for copy in halo_c[:4]:
        copy.start()
    conv(band_f, xf, pb)

    def core_copy(g):
        part = pl.ds(3 * g, 3)
        return remote(c_send.at[part], c_recv.at[part], c_ss.at[g], c_rs.at[g], dev_core)

    for g in range(3):
        parts = [mm(cot_t[g % 2], pb[k]) for k in range(3 * g, 3 * g + 3)]
        for m, part in enumerate(parts):
            c_send[3 * g + m] = part[0:128].astype(BF)
        core_copy(g).start()
        for m, part in enumerate(parts):
            g_own[3 * g + m] = part[128:256]

    def xa_copy(s, g):
        part = pl.ds(3 * g, 3)
        return remote(
            xa_send.at[s - 1, part], xa_recv.at[s - 1, part], xa_ss.at[s - 1, g], xa_rs.at[s - 1, g], dev_x(s)
        )

    def zb_copy(s):
        return remote(zb_send.at[s - 1], zb_recv.at[s - 1], zb_ss.at[s - 1], zb_rs.at[s - 1], dev_z(s))

    for g in range(3):
        core_copy(g).wait_recv()
        for m in range(3):
            k = 3 * g + m
            total = g_own[k] + c_recv[k].astype(F32)
            if g == 1:
                zb_own[m] = total[0:16]
                for s in range(1, NZ):
                    zb_send[s - 1, m] = total[16 * s : 16 * s + 16].astype(BF)
            else:
                at = 3 * (g // 2) + m
                xa_own[at] = total[0:32]
                for s in range(1, NX):
                    xa_send[s - 1, at] = total[32 * s : 32 * s + 32].astype(BF)
        if g == 1:
            for s in FAR8:
                zb_copy(s).start()
        else:
            for s in FAR4:
                xa_copy(s, g // 2).start()

    loads[4].wait()
    mixed = mm_nt(pb[0], wv[0])
    for k in range(1, KB):
        mixed = mixed + mm_nt(pb[k], wv[k])
    both_ref[0] = mm(join_own, mixed.astype(BF)).astype(BF).reshape(JC, 2, CH)

    def za_copy(s):
        return remote(za_send.at[s - 1], za_recv.at[s - 1], za_ss.at[s - 1], za_rs.at[s - 1], dev_z(s))

    def xb_copy(s):
        return remote(xb_send.at[s - 1], xb_recv.at[s - 1], xb_ss.at[s - 1], xb_rs.at[s - 1], dev_x(s))

    for g in range(2):
        for s in range(1, NX):
            xa_copy(s, g).wait_recv()
        for at in range(3 * g, 3 * g + 3):
            total = xa_own[at]
            for s in range(1, NX):
                total = total + xa_recv[s - 1, at].astype(F32)
            for h in range(2):
                za_f32[pl.ds(2 * at + h, 32, stride=12), :] = total[:, 128 * h : 128 * h + 128]
    for s in FAR8:
        za_send[s - 1] = za_f32[48 * s : 48 * s + 48, :].astype(BF)
        za_copy(s).start()
    for s in range(1, NZ):
        zb_copy(s).wait_recv()
    for m in range(3):
        total = zb_own[m]
        for s in range(1, NZ):
            total = total + zb_recv[s - 1, m].astype(F32)
        for h in range(2):
            xb_f32[pl.ds(2 * m + h, 16, stride=6), :] = total[:, 128 * h : 128 * h + 128]
    for s in FAR4:
        xb_send[s - 1, 0:24, :] = xb_f32[24 * s : 24 * s + 24, :].astype(BF)
        xb_send[s - 1, 24:32, :] = jnp.zeros((8, 128), BF)
        xb_copy(s).start()

    def y_copy(s):
        return remote(y_send.at[s - 1], y_recv.at[s - 1], y_ss.at[s - 1], y_rs.at[s - 1], dev_y(s))

    for copy in halo_c[:4]:
        copy.wait_recv()
    for copy in halo_c[4:]:
        copy.start()

    total = xb_f32[0:24, :]
    for s in NEAR4:
        xb_copy(s).wait_recv()
        total = total + xb_recv[s - 1, 0:24, :].astype(F32)
    yb_f32[...] = total
    total = za_f32[0:48, :]
    for s in NEAR8:
        za_copy(s).wait_recv()
        total = total + za_recv[s - 1].astype(F32)
    ya_f32[...] = total

    def y_rows(to):
        return [ya_f32[pl.ds(6 * to, 6), :], yb_f32[pl.ds(3 * to, 3), :]]

    for s in FAR8:
        rows = y_rows((y + s) % NY)
        y_send[s - 1] = jnp.concatenate(rows + [jnp.zeros((7, 128), F32)], axis=0).astype(BF)
        y_copy(s).start()
    for copy in halo_c[4:]:
        copy.wait_recv()
    conv(band_b, xc, sb)
    grad = mm(sb[0], wv[0])
    for k in range(1, KB):
        grad = grad + mm(sb[k], wv[k])
    both_ref[1] = mm(join_own, grad.astype(BF)).astype(BF).reshape(JC, 2, CH)

    total = jnp.concatenate(y_rows(y), axis=0)
    for s in NEAR8:
        y_copy(s).wait_recv()
        total = total + y_recv[s - 1].astype(F32)[0:9]
    total = jnp.where(y % 2 == 0, total, jnp.concatenate([total[6:9], total[0:6]], axis=0))
    wg_ref[...] = total * (1.0 / math.sqrt(2 * NLAT_AX * JC * NLON_AX))

    for copy in halo_f + halo_c:
        copy.wait_send()
    for g in range(3):
        core_copy(g).wait_send()
    for s in range(1, NX):
        xa_copy(s, 0).wait_send()
        xa_copy(s, 1).wait_send()
        xb_copy(s).wait_send()
    for s in range(1, NZ):
        zb_copy(s).wait_send()
        za_copy(s).wait_send()
    for s in range(1, NY):
        y_copy(s).wait_send()


def local(fields, basis, half_width, weight, cotangent):
    dma = pltpu.SemaphoreType.DMA
    vmem = pltpu.VMEM
    hbm_spec = pl.BlockSpec(memory_space=pltpu.HBM)
    vm_spec = pl.BlockSpec(memory_space=pltpu.VMEM)
    both, wg = pl.pallas_call(
        kernel,
        out_shape=(jax.ShapeDtypeStruct((2, JC, 2, CH), BF), jax.ShapeDtypeStruct((9, 128), F32)),
        in_specs=[hbm_spec] * 5,
        out_specs=(vm_spec,) * 2,
        scratch_shapes=[
            vmem((JC, 2, CH), BF), vmem((JC, 2, CH), BF), vmem((27 * 64, 128), BF),
            pltpu.SMEM((64,), jnp.int32), vmem((KB, CH, CH), BF),
            vmem((2, HALO, CH), BF), vmem((2, HALO, CH), BF),
            vmem((4, 256, CH), BF), vmem((4, 256, CH), BF),
            vmem((64, 128), F32), vmem((64, 128), F32),
            vmem((2, KB * JP, 768), BF), vmem((2, KB * JP, 768), BF), vmem((6, JP, 128), BF),
            vmem((KB, 2 * JP, CH), BF), vmem((KB, 2 * JP, CH), BF), vmem((2, CH, 2 * JP), BF),
            vmem((KB, 128, CH), F32), vmem((KB, 128, CH), BF), vmem((KB, 128, CH), BF),
            vmem((6, 32, CH), F32), vmem((3, 6, 32, CH), BF), vmem((3, 6, 32, CH), BF),
            vmem((3, 16, CH), F32), vmem((7, 3, 16, CH), BF), vmem((7, 3, 16, CH), BF),
            vmem((32 * 12, 128), F32), vmem((7, 48, 128), BF), vmem((7, 48, 128), BF),
            vmem((16 * 6, 128), F32), vmem((3, 32, 128), BF), vmem((3, 32, 128), BF),
            vmem((48, 128), F32), vmem((24, 128), F32), vmem((7, 16, 128), BF), vmem((7, 16, 128), BF),
            dma((5,)), dma((16,)), dma((16,)), dma((3,)), dma((3,)), dma((3, 2)), dma((3, 2)),
            dma((7,)), dma((7,)), dma((7,)), dma((7,)), dma((3,)), dma((3,)), dma((7,)), dma((7,)),
        ],
        compiler_params=pltpu.CompilerParams(
            collective_id=0, has_side_effects=True, vmem_limit_bytes=48 * 1024 * 1024
        ),
    )(
        *[
            pltpu.with_memory_space_constraint(a, pltpu.HBM)
            for a in (
                jnp.transpose(fields, (2, 1, 0)),
                jnp.transpose(basis, (1, 2, 0, 3)).reshape(27 * 64, 128),
                half_width,
                jnp.transpose(weight, (1, 0, 2)),
                jnp.transpose(cotangent, (2, 1, 0)),
            )
        ]
    )
    return jnp.transpose(both[0], (2, 1, 0)), jnp.transpose(both[1], (2, 1, 0)), wg.reshape(-1)


def solution(mesh):
    placed = (P(None, "lat", "lon"), P(), P(), P(), P(None, "lat", "lon"))
    return jax.shard_map(
        local,
        mesh=mesh,
        in_specs=placed,
        out_specs=(P(None, "lat", "lon"), P(None, "lat", "lon"), P(("lat", "lon"))),
        check_vma=False,
    )
```

```python
import math

import jax
import jax.numpy as jnp
from jax import lax
from jax.experimental import pallas as pl
from jax.experimental.pallas import tpu as pltpu
from jax.sharding import PartitionSpec as P

MESH = pl.DeviceIdType.MESH
BF = jnp.bfloat16
F32 = jnp.float32

CH = 256
KB = 9
JC = 90
JP = 96
HALO = 64
NLAT_AX = 32
NLON_AX = 16
NX, NZ, NY = 4, 8, 8
FAR4 = (2, 1, 3)
FAR8 = (4, 3, 5, 2, 6, 1, 7)
NEAR4 = FAR4[::-1]
NEAR8 = FAR8[::-1]


def iota(shape, dim):
    return lax.broadcasted_iota(jnp.int32, shape, dim)


def onehot(cond):
    return jnp.where(cond, 1.0, 0.0).astype(BF)


def mm(a, b):
    return jnp.dot(a, b, preferred_element_type=F32)


def mm_nt(a, b):
    return lax.dot_general(a, b, (((1,), (1,)), ((), ())), preferred_element_type=F32)


def kernel(
    f_hbm, basis_hbm, hw_hbm, w_hbm, c_hbm,
    both_ref, wg_ref,
    fv, cv, bv, hw_ref, wv,
    f_last, c_last,
    xf, xc,
    base_f, base_b, band_f, band_b, masks,
    pb, sb, cot_t,
    g_own, c_send, c_recv,
    x_own, x_send, x_recv,
    z_f32, z_send, z_recv,
    y_f32, y_send, y_recv,
    in_sem, halo_ss, halo_rs, c_ss, c_rs, x_ss, x_rs, z_ss, z_rs, y_ss, y_rs,
):
    lat = lax.axis_index("lat")
    lon = lax.axis_index("lon")
    core = lat % 2
    zl = (lat // 2) % 4
    x = lat // 8
    zh = lon // 8
    y = lon % 8
    z = zh * 4 + zl
    i0 = lat * 2

    def dev_x(s):
        return (((x + s) % NX) * 8 + zl * 2 + core, lon)

    def dev_z(s):
        t = (z + s) % NZ
        return (x * 8 + (t % 4) * 2 + core, (t // 4) * 8 + y)

    def dev_y(s):
        return (lat, zh * 8 + (y + s) % NY)

    dev_core = (x * 8 + zl * 2 + (1 - core), lon)

    def near(up, right):
        return ((lat + NLAT_AX + up) % NLAT_AX, (lon + NLON_AX + right) % NLON_AX)

    barrier = pltpu.get_barrier_semaphore()
    peers = [near(u, r) for r in (-1, 1) for u in (-1, 0, 1)]
    for s in FAR8:
        peers += [dev_z(s), dev_y(s)]
    peers += [near(-1, 0), near(1, 0)]
    peers += [dev_x(s) for s in FAR4]
    peers += [dev_core]
    for peer in peers:
        pl.semaphore_signal(barrier, inc=1, device_id=peer, device_id_type=MESH)

    loads = [
        pltpu.make_async_copy(src, dst, in_sem.at[n])
        for n, (src, dst) in enumerate(
            ((f_hbm, fv), (c_hbm, cv), (basis_hbm, bv), (hw_hbm, hw_ref), (w_hbm, wv))
        )
    ]
    for load in loads:
        load.start()

    def remote(src, dst, ss, rs, dev):
        return pltpu.make_async_remote_copy(
            src_ref=src, dst_ref=dst, send_sem=ss, recv_sem=rs, device_id=dev, device_id_type=MESH
        )

    p = iota((320, 180), 0)
    r_own = (p >= JP).astype(jnp.int32)
    r_last = (p >= 256).astype(jnp.int32)
    want = jnp.where(p < 192, 2 * (p - JP * r_own) + r_own, 2 * (p - 192 - HALO * r_last + JC - HALO) + r_last)
    split = onehot(iota((320, 180), 1) == want)
    q192 = iota((180, 192), 1)
    s192 = (q192 >= JP).astype(jnp.int32)
    join_own = onehot(iota((180, 192), 0) == 2 * (q192 - JP * s192) + s192)

    def place(raw, buf, last):
        rows = mm(split, raw[...].reshape(180, CH)).astype(BF)
        buf[1, 0:JP, :] = rows[0:JP]
        buf[2, 0:JP, :] = rows[JP:192]
        last[0] = rows[192:256]
        last[1] = rows[256:320]
        for row in range(4):
            buf[row, JP:128, :] = jnp.zeros((128 - JP, CH), BF)

    both, own, first = pl.ds(1, 2), pl.ds(0, JP), pl.ds(0, HALO)
    left, right, sides = pl.ds(128, HALO), pl.ds(192, HALO), pl.ds(128, 2 * HALO)

    def halo_copies(n, buf, last):
        moves = (
            (last, buf.at[both, left], near(0, 1)),
            (buf.at[both, first], buf.at[both, right], near(0, -1)),
            (buf.at[2, own], buf.at[0, own], near(1, 0)),
            (buf.at[1, own], buf.at[3, own], near(-1, 0)),
        )
        if n == 0:
            moves += (
                (last.at[1], buf.at[0, left], near(1, 1)),
                (buf.at[2, first], buf.at[0, right], near(1, -1)),
                (last.at[0], buf.at[3, left], near(-1, 1)),
                (buf.at[1, first], buf.at[3, right], near(-1, -1)),
            )
        else:
            moves += (
                (buf.at[2, sides], buf.at[0, sides], near(1, 0)),
                (buf.at[1, sides], buf.at[3, sides], near(-1, 0)),
            )
        return [
            remote(src, dst, halo_ss.at[8 * n + m], halo_rs.at[8 * n + m], dev)
            for m, (src, dst, dev) in enumerate(moves)
        ]

    loads[0].wait()
    place(fv, xf, f_last)
    pl.semaphore_wait(barrier, len(peers))
    halo_f = halo_copies(0, xf, f_last)
    halo_c = halo_copies(1, xc, c_last)
    for copy in halo_f:
        copy.start()
    loads[1].wait()
    place(cv, xc, c_last)

    loads[2].wait()
    loads[3].wait()
    n_row = iota((64, 1), 0)
    r_row = (n_row >= 27).astype(jnp.int32)
    m_row = n_row - 27 * r_row
    d_row = (m_row >= 9).astype(jnp.int32) + (m_row >= 18).astype(jnp.int32)
    k_row = m_row - 9 * d_row
    col = iota((64, 27 * 64), 1)
    lane64 = iota((64, 128), 1)
    step = r_row + d_row
    row_of = i0 + step - 1
    outside = (row_of < 0) | (row_of > 63)
    target = (d_row * 9 + k_row) * 64 + i0 + r_row
    target = jnp.where(outside, -1, target)
    taps = mm(onehot(col == target), bv[...])
    width = jnp.where(r_row == 0, hw_ref[i0], hw_ref[i0 + 1])
    base_f[...] = jnp.where(jnp.abs(lane64 - HALO) <= width, taps, 0.0)
    target = ((2 - d_row) * 9 + k_row) * 64 + row_of
    target = jnp.where(outside, -1, target)
    taps = mm(onehot(col == target), bv[...])
    widths = [hw_ref[(i0 + 63 + s) % 64] for s in range(4)]
    width = jnp.where(
        step == 0, widths[0], jnp.where(step == 1, widths[1], jnp.where(step == 2, widths[2], widths[3]))
    )
    taps = jnp.where(jnp.abs(lane64 - HALO) <= width, taps, 0.0).astype(BF)
    turn = onehot((iota((128, 128), 0) + iota((128, 128), 1)) % 128 == 0)
    base_b[...] = mm(taps, turn)

    jj = iota((JP, 128), 0)
    ll = iota((JP, 128), 1)
    for low in range(2):
        idx = 64 + ll - jj
        masks[3 * low] = onehot((idx >= low) & (idx <= 127 + low))
        masks[3 * low + 1] = onehot((ll < HALO) & (ll - jj >= low))
        masks[3 * low + 2] = onehot((ll >= HALO) & (JC + ll - jj <= 127 + low))

    def build(base, band, low):
        def body(k, carry):
            at = pl.multiple_of(k * JP, JP)
            for r in range(2):
                for d in range(3):
                    row = base[pl.ds((r * 3 + d) * 9 + k, 1), :].astype(BF)
                    wide = jnp.broadcast_to(row, (JP, 128))
                    s0 = pltpu.roll(wide, 0, 1, stride=1, stride_axis=0)
                    s1 = pltpu.roll(s0, 64, 1)
                    s2 = pltpu.roll(s0, 38, 1)
                    band[r, pl.ds(at, JP), d * 256 : d * 256 + 128] = s1 * masks[3 * low]
                    band[r, pl.ds(at, JP), d * 256 + 128 : d * 256 + 256] = (
                        s0 * masks[3 * low + 1] + s2 * masks[3 * low + 2]
                    )
            return carry

        lax.fori_loop(0, KB, body, 0)

    build(base_f, band_f, 0)

    o_new = iota((256, 1), 0)
    mine = (o_new % 64) // 32
    to_x = ((o_new % 32) // 8 + x) % NX
    to_z = 2 * (o_new // 64) + (o_new % 8) // 4
    to_core = mine * core + (1 - mine) * (1 - core)
    o_old = to_x * 64 + (to_z % 4) * 16 + to_core * 8 + (to_z // 4) * 4 + o_new % 4
    order = onehot(iota((256, 256), 1) == o_old)
    cot_rows = jnp.concatenate([xc[1, 0:JP, :], xc[2, 0:JP, :]], axis=0)
    cot_t[...] = mm_nt(order, cot_rows).astype(BF)

    build(base_b, band_b, 1)

    def conv(band, buf, dst):
        for r in range(2):
            res = mm(band[r], buf[r : r + 3].reshape(768, CH)).astype(BF)
            for k in range(KB):
                dst[k, r * JP : (r + 1) * JP, :] = res[k * JP : (k + 1) * JP]

    for copy in halo_f:
        copy.wait_recv()
    for copy in halo_c[:4]:
        copy.start()
    conv(band_f, xf, pb)

    def core_copy(q):
        return remote(c_send.at[q], c_recv.at[q], c_ss.at[q], c_rs.at[q], dev_core)

    def x_copy(q, s):
        return remote(x_send.at[q, s - 1], x_recv.at[q, s - 1], x_ss.at[q, s - 1], x_rs.at[q, s - 1], dev_x(s))

    def grad_part(q):
        parts = [mm(cot_t[64 * q : 64 * q + 64], pb[k]) for k in range(KB)]
        for k, part in enumerate(parts):
            c_send[q, k] = part[0:32].astype(BF)
        core_copy(q).start()
        for k, part in enumerate(parts):
            g_own[q, k] = part[32:64]

    def core_sum(q):
        core_copy(q).wait_recv()
        totals = [g_own[q, k] + c_recv[q, k].astype(F32) for k in range(KB)]
        for s in FAR4:
            rows = [total[8 * s : 8 * s + 8] for total in totals] + [jnp.zeros((8, CH), F32)]
            x_send[q, s - 1] = jnp.concatenate(rows, axis=0).astype(BF)
            x_copy(q, s).start()
        x_own[q] = jnp.concatenate([total[0:8] for total in totals], axis=0)

    grad_part(0)
    grad_part(1)
    core_sum(0)
    grad_part(2)
    core_sum(1)
    grad_part(3)
    core_sum(2)
    core_sum(3)

    loads[4].wait()
    mixed = mm_nt(pb[0], wv[0])
    for k in range(1, KB):
        mixed = mixed + mm_nt(pb[k], wv[k])
    both_ref[0] = mm(join_own, mixed.astype(BF)).astype(BF).reshape(JC, 2, CH)

    def z_copy(to):
        slot = (z + NZ - 1 - to) % NZ
        dev = (x * 8 + (to % 4) * 2 + core, (to // 4) * 8 + y)
        return remote(z_send.at[to], z_recv.at[slot], z_ss.at[to], z_rs.at[slot], dev)

    def x_sum(q):
        total = x_own[q]
        for s in NEAR4:
            x_copy(q, s).wait_recv()
            total = total + x_recv[q, s - 1, 0:72, :].astype(F32)
        for k in range(KB):
            for h in range(2):
                z_f32[q, pl.ds(2 * k + h, 8, stride=18), :] = total[8 * k : 8 * k + 8, 128 * h : 128 * h + 128]
        for to in (2 * q, 2 * q + 1):
            at = 72 * (to % 2)
            z_send[to, 0:72, :] = z_f32[q, at : at + 72, :].astype(BF)
            z_send[to, 72:80, :] = jnp.zeros((8, 128), BF)

            @pl.when(z != to)
            def _(to=to):
                z_copy(to).start()

    x_sum(0)
    x_sum(1)
    for copy in halo_c[:4]:
        copy.wait_recv()
    for copy in halo_c[4:]:
        copy.start()

    x_sum(2)
    x_sum(3)

    def y_copy(s):
        return remote(y_send.at[s - 1], y_recv.at[s - 1], y_ss.at[s - 1], y_rs.at[s - 1], dev_y(s))

    total = z_f32[z // 2, pl.ds(pl.multiple_of(72 * (z % 2), 8), 72), :]
    for s in NEAR8:
        remote(z_send.at[0], z_recv.at[s - 1], z_ss.at[0], z_rs.at[s - 1], dev_z(s)).wait_recv()
        total = total + z_recv[s - 1, 0:72, :].astype(F32)
    y_f32[...] = total

    for s in FAR8:
        rows = y_f32[pl.ds(9 * ((y + s) % NY), 9), :]
        y_send[s - 1] = jnp.concatenate([rows, jnp.zeros((7, 128), F32)], axis=0).astype(BF)
        y_copy(s).start()
    for copy in halo_c[4:]:
        copy.wait_recv()
    conv(band_b, xc, sb)
    grad = mm(sb[0], wv[0])
    for k in range(1, KB):
        grad = grad + mm(sb[k], wv[k])
    both_ref[1] = mm(join_own, grad.astype(BF)).astype(BF).reshape(JC, 2, CH)

    total = y_f32[pl.ds(9 * y, 9), :]
    for s in NEAR8:
        y_copy(s).wait_recv()
        total = total + y_recv[s - 1].astype(F32)[0:9]
    wg_ref[...] = total * (1.0 / math.sqrt(2 * NLAT_AX * JC * NLON_AX))

    for copy in halo_f + halo_c:
        copy.wait_send()
    for q in range(4):
        core_copy(q).wait_send()
        for s in range(1, NX):
            x_copy(q, s).wait_send()
    for to in range(NZ):

        @pl.when(z != to)
        def _(to=to):
            z_copy(to).wait_send()

    for s in range(1, NY):
        y_copy(s).wait_send()


def local(fields, basis, half_width, weight, cotangent):
    dma = pltpu.SemaphoreType.DMA
    vmem = pltpu.VMEM
    hbm_spec = pl.BlockSpec(memory_space=pltpu.HBM)
    vm_spec = pl.BlockSpec(memory_space=pltpu.VMEM)
    both, wg = pl.pallas_call(
        kernel,
        out_shape=(jax.ShapeDtypeStruct((2, JC, 2, CH), BF), jax.ShapeDtypeStruct((9, 128), F32)),
        in_specs=[hbm_spec] * 5,
        out_specs=(vm_spec,) * 2,
        scratch_shapes=[
            vmem((JC, 2, CH), BF), vmem((JC, 2, CH), BF), vmem((27 * 64, 128), BF),
            pltpu.SMEM((64,), jnp.int32), vmem((KB, CH, CH), BF),
            vmem((2, HALO, CH), BF), vmem((2, HALO, CH), BF),
            vmem((4, 256, CH), BF), vmem((4, 256, CH), BF),
            vmem((64, 128), F32), vmem((64, 128), F32),
            vmem((2, KB * JP, 768), BF), vmem((2, KB * JP, 768), BF), vmem((6, JP, 128), BF),
            vmem((KB, 2 * JP, CH), BF), vmem((KB, 2 * JP, CH), BF), vmem((CH, 2 * JP), BF),
            vmem((4, KB, 32, CH), F32), vmem((4, KB, 32, CH), BF), vmem((4, KB, 32, CH), BF),
            vmem((4, 72, CH), F32), vmem((4, 3, 80, CH), BF), vmem((4, 3, 80, CH), BF),
            vmem((4, 144, 128), F32), vmem((8, 80, 128), BF), vmem((8, 80, 128), BF),
            vmem((72, 128), F32), vmem((7, 16, 128), BF), vmem((7, 16, 128), BF),
            dma((5,)), dma((16,)), dma((16,)), dma((4,)), dma((4,)), dma((4, 3)), dma((4, 3)),
            dma((8,)), dma((8,)), dma((7,)), dma((7,)),
        ],
        compiler_params=pltpu.CompilerParams(
            collective_id=0, has_side_effects=True, vmem_limit_bytes=48 * 1024 * 1024
        ),
    )(
        *[
            pltpu.with_memory_space_constraint(a, pltpu.HBM)
            for a in (
                jnp.transpose(fields, (2, 1, 0)),
                jnp.transpose(basis, (1, 2, 0, 3)).reshape(27 * 64, 128),
                half_width,
                jnp.transpose(weight, (1, 0, 2)),
                jnp.transpose(cotangent, (2, 1, 0)),
            )
        ]
    )
    return jnp.transpose(both[0], (2, 1, 0)), jnp.transpose(both[1], (2, 1, 0)), wg.reshape(-1)


def solution(mesh):
    placed = (P(None, "lat", "lon"), P(), P(), P(), P(None, "lat", "lon"))
    return jax.shard_map(
        local,
        mesh=mesh,
        in_specs=placed,
        out_specs=(P(None, "lat", "lon"), P(None, "lat", "lon"), P(("lat", "lon"))),
        check_vma=False,
    )
```

```python
import math

import jax
import jax.numpy as jnp
from jax import lax
from jax.experimental import pallas as pl
from jax.experimental.pallas import tpu as pltpu
from jax.sharding import PartitionSpec as P

MESH = pl.DeviceIdType.MESH
BF = jnp.bfloat16
F32 = jnp.float32

CH = 256
KB = 9
JC = 90
JP = 96
HALO = 64
NLAT_AX = 32
NLON_AX = 16
NX, NZ, NY = 4, 8, 8
FAR4 = (2, 1, 3)
FAR8 = (4, 3, 5, 2, 6, 1, 7)
NEAR4 = FAR4[::-1]
NEAR8 = FAR8[::-1]


def iota(shape, dim):
    return lax.broadcasted_iota(jnp.int32, shape, dim)


def onehot(cond):
    return jnp.where(cond, 1.0, 0.0).astype(BF)


def mm(a, b):
    return jnp.dot(a, b, preferred_element_type=F32)


def mm_nt(a, b):
    return lax.dot_general(a, b, (((1,), (1,)), ((), ())), preferred_element_type=F32)


def kernel(
    f_hbm, basis_hbm, hw_hbm, w_hbm, c_hbm,
    both_ref, wg_ref,
    fv, cv, bv, hw_ref, wv,
    f_last, c_last,
    xf, xc,
    base_f, base_b, band_f, band_b, masks,
    pb, sb, cot_t,
    g_own, c_send, c_recv,
    x_own, x_send, x_recv,
    z_f32, z_send, z_recv,
    y_f32, y_send, y_recv,
    in_sem, halo_ss, halo_rs, c_ss, c_rs, x_ss, x_rs, z_ss, z_rs, y_ss, y_rs,
):
    lat = lax.axis_index("lat")
    lon = lax.axis_index("lon")
    core = lat % 2
    zl = (lat // 2) % 4
    x = lat // 8
    zh = lon // 8
    y = lon % 8
    z = zh * 4 + zl
    i0 = lat * 2

    def dev_x(s):
        return (((x + s) % NX) * 8 + zl * 2 + core, lon)

    def dev_z(s):
        t = (z + s) % NZ
        return (x * 8 + (t % 4) * 2 + core, (t // 4) * 8 + y)

    def dev_y(s):
        return (lat, zh * 8 + (y + s) % NY)

    dev_core = (x * 8 + zl * 2 + (1 - core), lon)

    def near(up, right):
        return ((lat + NLAT_AX + up) % NLAT_AX, (lon + NLON_AX + right) % NLON_AX)

    barrier = pltpu.get_barrier_semaphore()
    peers = [near(u, r) for r in (-1, 1) for u in (-1, 0, 1)]
    for s in FAR8:
        peers += [dev_z(s), dev_y(s)]
    peers += [near(-1, 0), near(1, 0)]
    peers += [dev_x(s) for s in FAR4]
    peers += [dev_core]
    for peer in peers:
        pl.semaphore_signal(barrier, inc=1, device_id=peer, device_id_type=MESH)

    loads = [
        pltpu.make_async_copy(src, dst, in_sem.at[n])
        for n, (src, dst) in enumerate(
            ((f_hbm, fv), (c_hbm, cv), (basis_hbm, bv), (hw_hbm, hw_ref), (w_hbm, wv))
        )
    ]
    for load in loads:
        load.start()

    def remote(src, dst, ss, rs, dev):
        return pltpu.make_async_remote_copy(
            src_ref=src, dst_ref=dst, send_sem=ss, recv_sem=rs, device_id=dev, device_id_type=MESH
        )

    p = iota((320, 180), 0)
    r_own = (p >= JP).astype(jnp.int32)
    r_last = (p >= 256).astype(jnp.int32)
    want = jnp.where(p < 192, 2 * (p - JP * r_own) + r_own, 2 * (p - 192 - HALO * r_last + JC - HALO) + r_last)
    split = onehot(iota((320, 180), 1) == want)
    q192 = iota((180, 192), 1)
    s192 = (q192 >= JP).astype(jnp.int32)
    join_own = onehot(iota((180, 192), 0) == 2 * (q192 - JP * s192) + s192)

    def place(raw, buf, last):
        rows = mm(split, raw[...].reshape(180, CH)).astype(BF)
        buf[1, 0:JP, :] = rows[0:JP]
        buf[2, 0:JP, :] = rows[JP:192]
        last[0] = rows[192:256]
        last[1] = rows[256:320]
        for row in range(4):
            buf[row, JP:128, :] = jnp.zeros((128 - JP, CH), BF)

    both, own, first = pl.ds(1, 2), pl.ds(0, JP), pl.ds(0, HALO)
    left, right, sides = pl.ds(128, HALO), pl.ds(192, HALO), pl.ds(128, 2 * HALO)

    def halo_copies(n, buf, last):
        moves = (
            (last, buf.at[both, left], near(0, 1)),
            (buf.at[both, first], buf.at[both, right], near(0, -1)),
            (buf.at[2, own], buf.at[0, own], near(1, 0)),
            (buf.at[1, own], buf.at[3, own], near(-1, 0)),
        )
        if n == 0:
            moves += (
                (last.at[1], buf.at[0, left], near(1, 1)),
                (buf.at[2, first], buf.at[0, right], near(1, -1)),
                (last.at[0], buf.at[3, left], near(-1, 1)),
                (buf.at[1, first], buf.at[3, right], near(-1, -1)),
            )
        else:
            moves += (
                (buf.at[2, sides], buf.at[0, sides], near(1, 0)),
                (buf.at[1, sides], buf.at[3, sides], near(-1, 0)),
            )
        return [
            remote(src, dst, halo_ss.at[8 * n + m], halo_rs.at[8 * n + m], dev)
            for m, (src, dst, dev) in enumerate(moves)
        ]

    loads[0].wait()
    place(fv, xf, f_last)
    pl.semaphore_wait(barrier, len(peers))
    halo_f = halo_copies(0, xf, f_last)
    halo_c = halo_copies(1, xc, c_last)
    for copy in halo_f:
        copy.start()
    loads[1].wait()
    place(cv, xc, c_last)

    loads[2].wait()
    loads[3].wait()
    n_row = iota((64, 1), 0)
    r_row = (n_row >= 27).astype(jnp.int32)
    m_row = n_row - 27 * r_row
    d_row = (m_row >= 9).astype(jnp.int32) + (m_row >= 18).astype(jnp.int32)
    k_row = m_row - 9 * d_row
    col = iota((64, 27 * 64), 1)
    lane64 = iota((64, 128), 1)
    step = r_row + d_row
    row_of = i0 + step - 1
    outside = (row_of < 0) | (row_of > 63)
    target = (d_row * 9 + k_row) * 64 + i0 + r_row
    target = jnp.where(outside, -1, target)
    taps = mm(onehot(col == target), bv[...])
    width = jnp.where(r_row == 0, hw_ref[i0], hw_ref[i0 + 1])
    base_f[...] = jnp.where(jnp.abs(lane64 - HALO) <= width, taps, 0.0)
    target = ((2 - d_row) * 9 + k_row) * 64 + row_of
    target = jnp.where(outside, -1, target)
    taps = mm(onehot(col == target), bv[...])
    widths = [hw_ref[(i0 + 63 + s) % 64] for s in range(4)]
    width = jnp.where(
        step == 0, widths[0], jnp.where(step == 1, widths[1], jnp.where(step == 2, widths[2], widths[3]))
    )
    taps = jnp.where(jnp.abs(lane64 - HALO) <= width, taps, 0.0).astype(BF)
    turn = onehot((iota((128, 128), 0) + iota((128, 128), 1)) % 128 == 0)
    base_b[...] = mm(taps, turn)

    jj = iota((JP, 128), 0)
    ll = iota((JP, 128), 1)
    for low in range(2):
        idx = 64 + ll - jj
        masks[3 * low] = onehot((idx >= low) & (idx <= 127 + low))
        masks[3 * low + 1] = onehot((ll < HALO) & (ll - jj >= low))
        masks[3 * low + 2] = onehot((ll >= HALO) & (JC + ll - jj <= 127 + low))

    def build(base, band, low):
        def body(k, carry):
            at = pl.multiple_of(k * JP, JP)
            for r in range(2):
                for d in range(3):
                    row = base[pl.ds((r * 3 + d) * 9 + k, 1), :].astype(BF)
                    wide = jnp.broadcast_to(row, (JP, 128))
                    s0 = pltpu.roll(wide, 0, 1, stride=1, stride_axis=0)
                    s1 = pltpu.roll(s0, 64, 1)
                    s2 = pltpu.roll(s0, 38, 1)
                    band[r, pl.ds(at, JP), d * 256 : d * 256 + 128] = s1 * masks[3 * low]
                    band[r, pl.ds(at, JP), d * 256 + 128 : d * 256 + 256] = (
                        s0 * masks[3 * low + 1] + s2 * masks[3 * low + 2]
                    )
            return carry

        lax.fori_loop(0, KB, body, 0)

    build(base_f, band_f, 0)

    o_new = iota((256, 1), 0)
    mine = (o_new % 64) // 32
    to_x = ((o_new % 32) // 8 + x) % NX
    to_z = 2 * (o_new // 64) + (o_new % 8) // 4
    to_core = mine * core + (1 - mine) * (1 - core)
    o_old = to_x * 64 + (to_z % 4) * 16 + to_core * 8 + (to_z // 4) * 4 + o_new % 4
    order = onehot(iota((256, 256), 1) == o_old)
    cot_rows = jnp.concatenate([xc[1, 0:JP, :], xc[2, 0:JP, :]], axis=0)
    cot_t[...] = mm_nt(order, cot_rows).astype(BF)

    build(base_b, band_b, 1)

    def conv(band, buf, dst):
        for r in range(2):
            res = mm(band[r], buf[r : r + 3].reshape(768, CH)).astype(BF)
            for k in range(KB):
                dst[k, r * JP : (r + 1) * JP, :] = res[k * JP : (k + 1) * JP]

    for copy in halo_f:
        copy.wait_recv()
    for copy in halo_c[:4]:
        copy.start()
    conv(band_f, xf, pb)

    def core_copy(q):
        return remote(c_send.at[q], c_recv.at[q], c_ss.at[q], c_rs.at[q], dev_core)

    def x_copy(q, s):
        return remote(x_send.at[q, s - 1], x_recv.at[q, s - 1], x_ss.at[q, s - 1], x_rs.at[q, s - 1], dev_x(s))

    def grad_part(q):
        parts = [mm(cot_t[64 * q : 64 * q + 64], pb[k]) for k in range(KB)]
        for k, part in enumerate(parts):
            c_send[q, k] = part[0:32].astype(BF)
        core_copy(q).start()
        for k, part in enumerate(parts):
            g_own[q, k] = part[32:64]

    def core_sum(q):
        core_copy(q).wait_recv()
        totals = [g_own[q, k] + c_recv[q, k].astype(F32) for k in range(KB)]
        for s in FAR4:
            rows = [total[8 * s : 8 * s + 8] for total in totals] + [jnp.zeros((8, CH), F32)]
            x_send[q, s - 1] = jnp.concatenate(rows, axis=0).astype(BF)
            x_copy(q, s).start()
        x_own[q] = jnp.concatenate([total[0:8] for total in totals], axis=0)

    grad_part(0)
    grad_part(1)
    core_sum(0)
    grad_part(2)
    core_sum(1)
    grad_part(3)
    core_sum(2)
    core_sum(3)

    loads[4].wait()
    mixed = mm_nt(pb[0], wv[0])
    for k in range(1, KB):
        mixed = mixed + mm_nt(pb[k], wv[k])
    both_ref[0] = mm(join_own, mixed.astype(BF)).astype(BF).reshape(JC, 2, CH)

    def y_copy(q, s):
        return remote(y_send.at[q, s - 1], y_recv.at[q, s - 1], y_ss.at[q, s - 1], y_rs.at[q, s - 1], dev_y(s))

    def y_rows(q, to):
        return [z_f32[q, pl.ds(9 * to, 9), :], z_f32[q, pl.ds(72 + 9 * to, 9), :]]

    def x_sum(q):
        total = x_own[q]
        for s in NEAR4:
            x_copy(q, s).wait_recv()
            total = total + x_recv[q, s - 1, 0:72, :].astype(F32)
        for k in range(KB):
            for h in range(2):
                z_f32[q, pl.ds(2 * k + h, 8, stride=18), :] = total[8 * k : 8 * k + 8, 128 * h : 128 * h + 128]
        for s in FAR8:
            rows = y_rows(q, (y + s) % NY) + [jnp.zeros((14, 128), F32)]
            y_send[q, s - 1] = jnp.concatenate(rows, axis=0).astype(BF)
            y_copy(q, s).start()

    def z_copy(to):
        slot = (z + NZ - 1 - to) % NZ
        dev = (x * 8 + (to % 4) * 2 + core, (to // 4) * 8 + y)
        return remote(z_send.at[to], z_recv.at[slot], z_ss.at[to], z_rs.at[slot], dev)

    def y_sum(q):
        total = jnp.concatenate(y_rows(q, y), axis=0)
        for s in NEAR8:
            y_copy(q, s).wait_recv()
            total = total + y_recv[q, s - 1].astype(F32)[0:18]
        for m in range(2):
            to = 2 * q + m
            rows = total[9 * m : 9 * m + 9]
            y_f32[to, 0:9, :] = rows
            z_send[to] = jnp.concatenate([rows, jnp.zeros((7, 128), F32)], axis=0).astype(BF)

            @pl.when(z != to)
            def _(to=to):
                z_copy(to).start()

    x_sum(0)
    x_sum(1)
    for copy in halo_c[:4]:
        copy.wait_recv()
    for copy in halo_c[4:]:
        copy.start()

    x_sum(2)
    y_sum(0)
    x_sum(3)
    y_sum(1)
    y_sum(2)
    y_sum(3)

    for copy in halo_c[4:]:
        copy.wait_recv()
    conv(band_b, xc, sb)
    grad = mm(sb[0], wv[0])
    for k in range(1, KB):
        grad = grad + mm(sb[k], wv[k])
    both_ref[1] = mm(join_own, grad.astype(BF)).astype(BF).reshape(JC, 2, CH)

    total = y_f32[z, 0:9, :]
    for s in NEAR8:
        remote(z_send.at[0], z_recv.at[s - 1], z_ss.at[0], z_rs.at[s - 1], dev_z(s)).wait_recv()
        total = total + z_recv[s - 1].astype(F32)[0:9]
    wg_ref[...] = total * (1.0 / math.sqrt(2 * NLAT_AX * JC * NLON_AX))

    for copy in halo_f + halo_c:
        copy.wait_send()
    for q in range(4):
        core_copy(q).wait_send()
        for s in range(1, NX):
            x_copy(q, s).wait_send()
        for s in range(1, NY):
            y_copy(q, s).wait_send()
    for to in range(NZ):

        @pl.when(z != to)
        def _(to=to):
            z_copy(to).wait_send()


def local(fields, basis, half_width, weight, cotangent):
    dma = pltpu.SemaphoreType.DMA
    vmem = pltpu.VMEM
    hbm_spec = pl.BlockSpec(memory_space=pltpu.HBM)
    vm_spec = pl.BlockSpec(memory_space=pltpu.VMEM)
    both, wg = pl.pallas_call(
        kernel,
        out_shape=(jax.ShapeDtypeStruct((2, JC, 2, CH), BF), jax.ShapeDtypeStruct((9, 128), F32)),
        in_specs=[hbm_spec] * 5,
        out_specs=(vm_spec,) * 2,
        scratch_shapes=[
            vmem((JC, 2, CH), BF), vmem((JC, 2, CH), BF), vmem((27 * 64, 128), BF),
            pltpu.SMEM((64,), jnp.int32), vmem((KB, CH, CH), BF),
            vmem((2, HALO, CH), BF), vmem((2, HALO, CH), BF),
            vmem((4, 256, CH), BF), vmem((4, 256, CH), BF),
            vmem((64, 128), F32), vmem((64, 128), F32),
            vmem((2, KB * JP, 768), BF), vmem((2, KB * JP, 768), BF), vmem((6, JP, 128), BF),
            vmem((KB, 2 * JP, CH), BF), vmem((KB, 2 * JP, CH), BF), vmem((CH, 2 * JP), BF),
            vmem((4, KB, 32, CH), F32), vmem((4, KB, 32, CH), BF), vmem((4, KB, 32, CH), BF),
            vmem((4, 72, CH), F32), vmem((4, 3, 80, CH), BF), vmem((4, 3, 80, CH), BF),
            vmem((4, 144, 128), F32), vmem((8, 16, 128), BF), vmem((8, 16, 128), BF),
            vmem((8, 16, 128), F32), vmem((4, 7, 32, 128), BF), vmem((4, 7, 32, 128), BF),
            dma((5,)), dma((16,)), dma((16,)), dma((4,)), dma((4,)), dma((4, 3)), dma((4, 3)),
            dma((8,)), dma((8,)), dma((4, 7)), dma((4, 7)),
        ],
        compiler_params=pltpu.CompilerParams(
            collective_id=0, has_side_effects=True, vmem_limit_bytes=48 * 1024 * 1024
        ),
    )(
        *[
            pltpu.with_memory_space_constraint(a, pltpu.HBM)
            for a in (
                jnp.transpose(fields, (2, 1, 0)),
                jnp.transpose(basis, (1, 2, 0, 3)).reshape(27 * 64, 128),
                half_width,
                jnp.transpose(weight, (1, 0, 2)),
                jnp.transpose(cotangent, (2, 1, 0)),
            )
        ]
    )
    return jnp.transpose(both[0], (2, 1, 0)), jnp.transpose(both[1], (2, 1, 0)), wg.reshape(-1)


def solution(mesh):
    placed = (P(None, "lat", "lon"), P(), P(), P(), P(None, "lat", "lon"))
    return jax.shard_map(
        local,
        mesh=mesh,
        in_specs=placed,
        out_specs=(P(None, "lat", "lon"), P(None, "lat", "lon"), P(("lat", "lon"))),
        check_vma=False,
    )
```
